256 devices in a mesh: row: 32 (over z_lo, x, core), col: 8 (over y, z_hi).
Axes of the slice: x: 4, y: 4, z: 8 (z_hi: 2, z_lo: 4; z = z_hi * 4 + z_lo), core: 2. Of those that a mesh axis runs over, the one named last changes fastest.
Arguments:
- layer_input: bfloat16 [2048, 16384], P('row', 'col'), may hold values from -6 to 6
- out_grad: bfloat16 [2048, 26624], P('row', 'col'), may hold values from -6 to 6
- up_weight: bfloat16 [16384, 26624], P('row', 'col'), may hold values from -0.046875 to 0.046875
Outputs:
- input_grad: bfloat16 [2048, 16384], P('row', 'col')
- weight_grad: float32 [16384, 26624], P('row', 'col')
The draws below stay inside these ranges and needn't reach their ends.
All inputs are finite; a program needn't handle non-finite values.
Results may differ from the reference program's by a relative error of at most 0.0012.
Values may be sent and summed in bfloat16 or wider, within the bound.
No kernel may reach another device: no remote copies, remote signals or barrier semaphores. Data moves between devices by JAX's collectives and lax.ppermute only.
A program may use at most 128 MiB of HBM per device.

```python
import math
import jax
import jax.numpy as jnp

D = 16384
FF_WIN = 26624
TOKENS = 2048


def shard_levels(stream_key, extent, shards, least, largest):
    def one(position, blocks):
        heights = jax.random.uniform(jax.random.fold_in(jax.random.fold_in(stream_key, 6), position), (blocks,), jnp.float32, least / len(shards), largest / len(shards))
        return jnp.repeat(jnp.exp(heights), extent[position] // blocks).reshape((-1,) + (1,) * (len(extent) - position - 1))

    level = one(*shards[0])
    for cut in shards[1:]:
        level = level * one(*cut)
    return level


def bell_draw(stream_key, extent, spread, limit, split=(), held_as=jnp.bfloat16):
    array = jax.random.normal(stream_key, extent, jnp.float32) * spread
    if len(split) > 0:
        array = shard_levels(stream_key, extent, split, -0.22, 0.18) * array
    return jnp.clip(array, min=-limit, max=limit).astype(held_as)


def setup_inputs(seed: int = 0) -> dict:
    streams_of = jax.random.split(jax.random.key(seed), 4)
    return {
        "layer_input": bell_draw(streams_of[0], (TOKENS, D), 1.0, 6.0, ((0, 32), (1, 8))),
        "out_grad": bell_draw(streams_of[1], (TOKENS, FF_WIN), 1.0, 6.0, ((0, 32), (1, 8))),
        "up_weight": bell_draw(streams_of[2], (D, FF_WIN), D ** -0.5, 0.046875, ((0, 32), (1, 8))),
    }


def reference(layer_input, out_grad, up_weight):
    input_grad = jnp.dot(out_grad, up_weight.T, preferred_element_type=jnp.float32).astype(jnp.bfloat16)
    weight_grad = jnp.dot(layer_input.T, out_grad, preferred_element_type=jnp.float32) * (1.0 / math.sqrt(TOKENS))
    return (input_grad, weight_grad)
```

```python
import math

import jax
import jax.numpy as jnp
from jax import lax
from jax.sharding import PartitionSpec as P

CHUNKS = (16, 16, 16, 16)


def perm_of(f):
    pairs = []
    for z in range(4):
        for x in range(4):
            for k in range(2):
                for y in range(4):
                    for h in range(2):
                        z2, x2, k2, y2, h2 = f(z, x, k, y, h)
                        src = (z * 8 + x * 2 + k) * 8 + y * 2 + h
                        dst = (z2 % 4 * 8 + x2 % 4 * 2 + k2) * 8 + y2 % 4 * 2 + h2
                        pairs.append((src, dst))
    return pairs


def move(a, f):
    return lax.ppermute(a, ("row", "col"), perm_of(f))


def to_z(a, d):
    return move(a, lambda z, x, k, y, h: (z + d, x, k, y, h))


def to_x(a, d):
    return move(a, lambda z, x, k, y, h: (z, x + d, k, y, h))


def to_y(a, d):
    return move(a, lambda z, x, k, y, h: (z, x, k, y + d, h))


def to_core(a):
    return move(a, lambda z, x, k, y, h: (z, x, 1 - k, y, h))


def to_h(a):
    return move(a, lambda z, x, k, y, h: (z, x, k, y, 1 - h))


def swap(a, dv, e):
    return move(a, lambda z, x, k, y, h: (y, 2 * h + ((x & 1) ^ dv), k ^ e, z, x >> 1))


def local(layer_input, out_grad, up_weight):
    row = lax.axis_index("row")
    col = lax.axis_index("col")
    z, x, core = row // 8, row // 2 % 4, row % 2
    xh, xl = x // 2, x % 2
    y, h = col // 2, col % 2
    same = xh == h
    near = same == (xl == 1)
    tokens, feats = layer_input.shape
    sub = feats // 4

    pieces = layer_input.reshape(tokens, 4, sub)
    got = []
    for dv in range(2):
        for e in range(2):
            f = (xl ^ dv) * 2 + (core ^ e)
            got.append(swap(lax.dynamic_index_in_dim(pieces, f, 1, keepdims=False), dv, e))
    mine = jnp.stack(got).reshape(2, 2, tokens, sub)
    other = to_h(mine)
    slab = jnp.stack(
        [
            jnp.where(same, mine[0], other[0]),
            jnp.where(near, mine[1], other[1]),
            jnp.where(same, other[0], mine[0]),
            jnp.where(near, other[1], mine[1]),
        ]
    )
    slab_up = to_y(slab, -1)
    slab_down = to_y(slab, 1)
    slab_far = jnp.concatenate([to_y(slab_up[:2], -1), to_y(slab_down[2:], 1)])
    slabs = jnp.stack([slab, slab_up, slab_far, slab_down])

    weight_grad = None
    kept = []
    at = 0
    for size in CHUNKS:
        g = out_grad[at : at + size]
        z1 = to_z(g, 1)
        z3 = to_z(g, -1)
        z2 = to_z(z1, 1)
        by_z = jnp.stack([g, z1, z2, z3])
        block = jnp.stack(
            [lax.dynamic_index_in_dim(by_z, (z - y - s) % 4, 0, keepdims=False) for s in range(4)]
        )
        x1 = to_x(block, 1)
        x3 = to_x(block, -1)
        x2 = jnp.concatenate([to_x(x1[:2], 1), to_x(x3[2:], -1)])
        near4 = (block, x1, x2, x3)
        all_g = jnp.stack([b for own in near4 for b in (own, to_core(own))])
        all_g = all_g.reshape(8 * 4 * size, -1)
        partial = lax.dot_general(
            all_g, up_weight, (((1,), (1,)), ((), ())), preferred_element_type=jnp.float32
        ).reshape(4, 2, 4, size, sub)
        mine = partial[:, :, 0]
        for s in range(1, 4):
            mine = mine + to_y(partial[:, :, s], s)
        keep = jnp.stack([jnp.where(same, mine[0], mine[2]), jnp.where(near, mine[1], mine[3])])
        send = jnp.stack([jnp.where(same, mine[2], mine[0]), jnp.where(near, mine[3], mine[1])])
        total = keep + to_h(send)
        kept.append(total.astype(jnp.bfloat16))
        rows = jnp.moveaxis(slabs[:, :, :, at : at + size], 0, 2).reshape(8 * 4 * size, sub)
        part = lax.dot_general(
            rows, all_g, (((0,), (0,)), ((), ())), preferred_element_type=jnp.float32
        )
        weight_grad = part if weight_grad is None else weight_grad + part
        at += size
    weight_grad = weight_grad * (1.0 / math.sqrt(tokens * 32))
    kept = jnp.concatenate(kept, axis=2)
    back = [swap(kept[dv, e], dv, e) for dv in range(2) for e in range(2)]
    input_grad = jnp.concatenate(
        [lax.dynamic_index_in_dim(jnp.stack(back), (xl ^ v) * 2 + (core ^ e), 0, keepdims=False)
         for v in range(2) for e in range(2)],
        axis=1,
    )
    return (input_grad, weight_grad)


def solution(mesh):
    in_specs = (P("row", "col"), P("row", "col"), P("row", "col"))
    out_specs = (P("row", "col"), P("row", "col"))
    return jax.shard_map(local, mesh=mesh, in_specs=in_specs, out_specs=out_specs, check_vma=False)
```

```python
import math

import jax
import jax.numpy as jnp
from jax import lax
from jax.experimental import pallas as pl
from jax.experimental.pallas import tpu as pltpu
from jax.sharding import PartitionSpec as P


def move(a, f):
    pairs = []
    for z in range(4):
        for x in range(4):
            for k in range(2):
                for y in range(4):
                    for h in range(2):
                        z2, x2, k2, y2, h2 = f(z, x, k, y, h)
                        src = (z * 8 + x * 2 + k) * 8 + y * 2 + h
                        dst = (z2 * 8 + x2 * 2 + k2) * 8 + y2 * 2 + h2
                        pairs.append((src, dst))
    return lax.ppermute(a, ("row", "col"), pairs)


def to_core(a):
    return move(a, lambda z, x, k, y, h: (z, x, 1 - k, y, h))


def to_h(a):
    return move(a, lambda z, x, k, y, h: (z, x, k, y, 1 - h))


FIRST, SECOND = (1, 3), (3, 1)


def to_y(a, step):
    return move(a, lambda z, x, k, y, h: (z, x, k, y ^ step[k], h))


def swap(a, dv):
    return move(a, lambda z, x, k, y, h: (y, 2 * h + ((x & 1) ^ dv), k, z ^ y, x >> 1))


def swap_back(a, dv):
    return move(a, lambda z, x, k, y, h: (z ^ y, 2 * h + ((x & 1) ^ dv), k, z, x >> 1))


def most_of(a):
    for f in (
        lambda z, x, k, y, h: (z, x, 1 - k, y, h),
        lambda z, x, k, y, h: (z, x ^ 1, k, y, h),
        lambda z, x, k, y, h: (z ^ 1, x, k, y, h),
        lambda z, x, k, y, h: (z, x, k, y ^ 1, h),
        lambda z, x, k, y, h: (z, x ^ 2, k, y, h),
        lambda z, x, k, y, h: (z ^ 2, x, k, y, h),
        lambda z, x, k, y, h: (z, x, k, y ^ 2, h),
        lambda z, x, k, y, h: (z, x, k, y, 1 - h),
    ):
        a = jnp.maximum(a, move(a, f))
    return a


def pick(a, i):
    return lax.dynamic_index_in_dim(a, i, 0, keepdims=False)


def pack(a, scale):
    return (a * scale).astype(jnp.float16)


def partial(grad, up_weight, order, tokens):
    step = tokens // 2
    n, k = up_weight.shape

    def kernel(order_ref, g_ref, w_ref, o_ref):
        o_ref[...] = lax.dot_general(
            g_ref[...], w_ref[...], (((1,), (1,)), ((), ())), preferred_element_type=jnp.float32
        )

    return pl.pallas_call(
        kernel,
        grid_spec=pltpu.PrefetchScalarGridSpec(
            num_scalar_prefetch=1,
            grid=(order.shape[0], 2),
            in_specs=[
                pl.BlockSpec((step, k), lambda i, j, order: (order[i] * 2 + j, 0)),
                pl.BlockSpec(memory_space=pltpu.VMEM),
            ],
            out_specs=pl.BlockSpec((step, n), lambda i, j, order: (i * 2 + j, 0)),
        ),
        out_shape=jax.ShapeDtypeStruct((order.shape[0] * tokens, n), jnp.float32),
        compiler_params=pltpu.CompilerParams(vmem_limit_bytes=54 * 1024 * 1024),
    )(order, grad, up_weight)


def local(layer_input, out_grad, up_weight):
    row = lax.axis_index("row")
    col = lax.axis_index("col")
    xl, core = row // 2 % 2, row % 2
    y, h = col // 2, col % 2
    first = core == 0
    own = row // 8 ^ y
    tokens, feats = layer_input.shape
    sub = feats // 4

    grad = lax.all_gather(out_grad, "row", axis=0, tiled=True)

    pieces = layer_input.reshape(tokens, 4, sub)
    piece = [
        [lax.dynamic_index_in_dim(pieces, 2 * v + (core ^ e), 1, keepdims=False) for e in range(2)]
        for v in range(2)
    ]
    mine = jnp.stack([piece[0][0], piece[1][0]])
    other = to_core(jnp.stack([piece[0][1], piece[1][1]]))
    both = jnp.where(first, jnp.stack([mine, other], 1), jnp.stack([other, mine], 1))
    got = [swap(pick(both, xl ^ dv), dv) for dv in range(2)]
    slab = jnp.stack([pick(jnp.stack(got), xl ^ v) for v in range(2)])
    slab = jnp.stack([slab, to_h(slab)])
    slab = jnp.stack([pick(slab, h ^ v) for v in range(2)])
    slab = jnp.stack([slab, to_y(slab, FIRST)])
    far = to_y(slab, SECOND)
    slab = jnp.stack(
        [slab[0], jnp.where(first, slab[1], far[0]), far[1], jnp.where(first, far[0], slab[1])]
    )
    slab = jnp.stack([pick(slab, own ^ v) for v in range(4)]).reshape(32 * tokens, sub)

    most = [jnp.max(jnp.abs(a)).astype(jnp.float32) for a in (out_grad, up_weight)]
    most = most_of(jnp.concatenate([jnp.broadcast_to(a, (8, 128)) for a in most]))
    most = most[:1, :1] * most[8:9, :1] * (4.0 * up_weight.shape[1])
    power = jnp.clip(14.0 - jnp.ceil(jnp.log2(most)), -126.0, 126.0)
    scale, back_scale = jnp.exp2(power), jnp.exp2(-power)

    grad, slab, scale = lax.optimization_barrier((grad, slab, scale))
    near = jnp.where(first, 1, 3)
    theirs = partial(grad, up_weight, jnp.stack([own ^ near, own ^ 2]), 8 * tokens)
    mine = partial(grad, up_weight, jnp.stack([own, own ^ near ^ 2]), 8 * tokens)

    def half(a, dv):
        a = a.reshape(2, 2, 2, 2 * tokens, sub)
        return lax.dynamic_index_in_dim(a, xl ^ dv, 2, keepdims=False)

    sums = []
    for dv in range(2):
        came = to_y(pack(half(theirs, dv), scale), FIRST).astype(jnp.float32) * back_scale
        keep = half(mine, dv) + came
        came = to_y(pack(keep[1], scale), SECOND).astype(jnp.float32) * back_scale
        sums.append(keep[0] + came)
    came = [to_h(pack(pick(a, 1 - h), scale)).astype(jnp.float32) * back_scale for a in sums]
    weight_grad = lax.dot_general(
        slab, grad, (((0,), (0,)), ((), ())), preferred_element_type=jnp.float32
    )
    weight_grad = weight_grad * (1.0 / math.sqrt(tokens * 32))
    back = []
    for dv in range(2):
        total = (pick(sums[dv], h) + came[dv]).astype(jnp.bfloat16).reshape(2, tokens, sub)
        other = to_core(pick(total, 1 - core))
        kept = pick(total, core)
        both = jnp.where(first, jnp.stack([kept, other]), jnp.stack([other, kept]))
        back.append(swap_back(both, dv))
    back = jnp.stack(back)
    back = jnp.stack([pick(back, xl ^ v) for v in range(2)])
    input_grad = jnp.concatenate([back[v, e] for v in range(2) for e in range(2)], axis=1)
    return (input_grad, weight_grad)


def solution(mesh):
    in_specs = (P("row", "col"), P("row", "col"), P("row", "col"))
    out_specs = (P("row", "col"), P("row", "col"))
    return jax.shard_map(local, mesh=mesh, in_specs=in_specs, out_specs=out_specs, check_vma=False)
```

```python
import math

import jax
import jax.numpy as jnp
from jax import lax
from jax.experimental import pallas as pl
from jax.experimental.pallas import tpu as pltpu
from jax.sharding import PartitionSpec as P


def move(a, f):
    pairs = []
    for z in range(4):
        for x in range(4):
            for k in range(2):
                for y in range(4):
                    for h in range(2):
                        z2, x2, k2, y2, h2 = f(z, x, k, y, h)
                        src = (z * 8 + x * 2 + k) * 8 + y * 2 + h
                        dst = (z2 * 8 + x2 * 2 + k2) * 8 + y2 * 2 + h2
                        pairs.append((src, dst))
    return lax.ppermute(a, ("row", "col"), pairs)


def to_core(a):
    return move(a, lambda z, x, k, y, h: (z, x, 1 - k, y, h))


def to_h(a):
    return move(a, lambda z, x, k, y, h: (z, x, k, y, 1 - h))


FIRST, SECOND = (1, 3), (3, 1)


def to_y(a, step):
    return move(a, lambda z, x, k, y, h: (z, x, k, y ^ step[k], h))


def swap(a, dv):
    return move(a, lambda z, x, k, y, h: (z ^ y, 2 * h + ((x & 1) ^ dv), k, y, x >> 1))


def swap_back(a, dv):
    return move(a, lambda z, x, k, y, h: (z ^ y, 2 * h + ((x & 1) ^ dv), k, z, x >> 1))


def most_of(a):
    for f in (
        lambda z, x, k, y, h: (z, x, 1 - k, y, h),
        lambda z, x, k, y, h: (z, x ^ 1, k, y, h),
        lambda z, x, k, y, h: (z ^ 1, x, k, y, h),
        lambda z, x, k, y, h: (z, x, k, y ^ 1, h),
        lambda z, x, k, y, h: (z, x ^ 2, k, y, h),
        lambda z, x, k, y, h: (z ^ 2, x, k, y, h),
        lambda z, x, k, y, h: (z, x, k, y ^ 2, h),
        lambda z, x, k, y, h: (z, x, k, y, 1 - h),
    ):
        a = jnp.maximum(a, move(a, f))
    return a


def pick(a, i):
    return lax.dynamic_index_in_dim(a, i, 0, keepdims=False)


def pack(a, scale):
    return (a * scale).astype(jnp.float16)


def partial(grad, up_weight, order, tokens):
    step = tokens // 2
    n, k = up_weight.shape

    def kernel(order_ref, g_ref, w_ref, o_ref):
        o_ref[...] = lax.dot_general(
            g_ref[...], w_ref[...], (((1,), (1,)), ((), ())), preferred_element_type=jnp.float32
        )

    return pl.pallas_call(
        kernel,
        grid_spec=pltpu.PrefetchScalarGridSpec(
            num_scalar_prefetch=1,
            grid=(order.shape[0], 2),
            in_specs=[
                pl.BlockSpec((step, k), lambda i, j, order: (order[i] * 2 + j, 0)),
                pl.BlockSpec(memory_space=pltpu.VMEM),
            ],
            out_specs=pl.BlockSpec((step, n), lambda i, j, order: (i * 2 + j, 0)),
        ),
        out_shape=jax.ShapeDtypeStruct((order.shape[0] * tokens, n), jnp.float32),
        compiler_params=pltpu.CompilerParams(vmem_limit_bytes=54 * 1024 * 1024),
    )(order, grad, up_weight)


def local(layer_input, out_grad, up_weight):
    row = lax.axis_index("row")
    col = lax.axis_index("col")
    xl, core = row // 2 % 2, row % 2
    y, h = col // 2, col % 2
    first = core == 0
    own = row // 8 ^ y
    tokens, feats = layer_input.shape
    sub = feats // 4

    grad = lax.all_gather(out_grad, "row", axis=0, tiled=True)

    pieces = layer_input.reshape(tokens, 4, sub)
    piece = [
        [lax.dynamic_index_in_dim(pieces, 2 * v + (core ^ e), 1, keepdims=False) for e in range(2)]
        for v in range(2)
    ]
    mine = jnp.stack([piece[0][0], piece[1][0]])
    other = to_core(jnp.stack([piece[0][1], piece[1][1]]))
    both = jnp.where(first, jnp.stack([mine, other], 1), jnp.stack([other, mine], 1))
    both = move(both, lambda z, x, k, y, h: (z, x, k, z ^ y, h))
    got = [swap(pick(both, xl ^ dv), dv) for dv in range(2)]
    slab = jnp.stack([pick(jnp.stack(got), xl ^ v) for v in range(2)])
    slab = jnp.stack([slab, to_h(slab)])
    slab = jnp.stack([pick(slab, h ^ v) for v in range(2)])
    slab = jnp.stack([slab, to_y(slab, FIRST)])
    far = to_y(slab, SECOND)
    slab = jnp.stack(
        [slab[0], jnp.where(first, slab[1], far[0]), far[1], jnp.where(first, far[0], slab[1])]
    )
    slab = jnp.stack([pick(slab, own ^ v) for v in range(4)]).reshape(32 * tokens, sub)

    most = [jnp.max(jnp.abs(a)).astype(jnp.float32) for a in (out_grad, up_weight)]
    most = most_of(jnp.concatenate([jnp.broadcast_to(a, (8, 128)) for a in most]))
    most = most[:1, :1] * most[8:9, :1] * (4.0 * up_weight.shape[1])
    power = jnp.clip(14.0 - jnp.ceil(jnp.log2(most)), -126.0, 126.0)
    scale, back_scale = jnp.exp2(power), jnp.exp2(-power)

    grad, slab, scale = lax.optimization_barrier((grad, slab, scale))
    near = jnp.where(first, 1, 3)
    theirs = partial(grad, up_weight, jnp.stack([own ^ near, own ^ 2]), 8 * tokens)
    mine = partial(grad, up_weight, jnp.stack([own, own ^ near ^ 2]), 8 * tokens)

    def half(a, dv):
        a = a.reshape(2, 2, 2, 2 * tokens, sub)
        return lax.dynamic_index_in_dim(a, xl ^ dv, 2, keepdims=False)

    sums = []
    for dv in range(2):
        came = to_y(pack(half(theirs, dv), scale), FIRST).astype(jnp.float32) * back_scale
        keep = half(mine, dv) + came
        came = to_y(pack(keep[1], scale), SECOND).astype(jnp.float32) * back_scale
        sums.append(keep[0] + came)
    came = [to_h(pack(pick(a, 1 - h), scale)).astype(jnp.float32) * back_scale for a in sums]
    weight_grad = lax.dot_general(
        slab, grad, (((0,), (0,)), ((), ())), preferred_element_type=jnp.float32
    )
    weight_grad = weight_grad * (1.0 / math.sqrt(tokens * 32))
    back = []
    for dv in range(2):
        total = (pick(sums[dv], h) + came[dv]).astype(jnp.bfloat16).reshape(2, tokens, sub)
        other = to_core(pick(total, 1 - core))
        kept = pick(total, core)
        both = jnp.where(first, jnp.stack([kept, other]), jnp.stack([other, kept]))
        back.append(swap_back(both, dv))
    back = jnp.stack(back)
    back = jnp.stack([pick(back, xl ^ v) for v in range(2)])
    input_grad = jnp.concatenate([back[v, e] for v in range(2) for e in range(2)], axis=1)
    return (input_grad, weight_grad)


def solution(mesh):
    in_specs = (P("row", "col"), P("row", "col"), P("row", "col"))
    out_specs = (P("row", "col"), P("row", "col"))
    return jax.shard_map(local, mesh=mesh, in_specs=in_specs, out_specs=out_specs, check_vma=False)
```

```python
import math

import jax
import jax.numpy as jnp
from jax import lax
from jax.experimental import pallas as pl
from jax.experimental.pallas import tpu as pltpu
from jax.sharding import PartitionSpec as P


def move(a, f):
    pairs = []
    for z in range(4):
        for x in range(4):
            for k in range(2):
                for y in range(4):
                    for h in range(2):
                        z2, x2, k2, y2, h2 = f(z, x, k, y, h)
                        src = (z * 8 + x * 2 + k) * 8 + y * 2 + h
                        dst = (z2 * 8 + x2 * 2 + k2) * 8 + y2 * 2 + h2
                        pairs.append((src, dst))
    return lax.ppermute(a, ("row", "col"), pairs)


def to_core(a):
    return move(a, lambda z, x, k, y, h: (z, x, 1 - k, y, h))


def to_h(a):
    return move(a, lambda z, x, k, y, h: (z, x, k, y, 1 - h))


FIRST, SECOND = (1, 3), (3, 1)


def to_y(a, step):
    return move(a, lambda z, x, k, y, h: (z, x, k, y ^ step[k], h))


def swap(a, dv):
    return move(a, lambda z, x, k, y, h: (z ^ y, 2 * h + ((x & 1) ^ dv), k, y, x >> 1))


def swap_back(a, dv):
    return move(a, lambda z, x, k, y, h: (z ^ y, 2 * h + ((x & 1) ^ dv), k, z, x >> 1))


ROUNDS = (
    lambda z, x, k, y, h: (z, x, 1 - k, y, h),
    lambda z, x, k, y, h: (z, x ^ 1, k, y, h),
    lambda z, x, k, y, h: (z, x, k, y ^ 1, h),
    lambda z, x, k, y, h: (z, x ^ 2, k, y, h),
    lambda z, x, k, y, h: (z, x, k, y ^ 2, h),
    lambda z, x, k, y, h: (z ^ 1, x, k, y, h),
    lambda z, x, k, y, h: (z ^ 2, x, k, y, h),
    lambda z, x, k, y, h: (z, x, k, y, 1 - h),
)


def most_of(a, rounds):
    for i in rounds:
        a = jnp.maximum(a, move(a, ROUNDS[i]))
    return a


def pick(a, i):
    return lax.dynamic_index_in_dim(a, i, 0, keepdims=False)


def pack(a, scale):
    return (a * scale).astype(jnp.float16)


def partial(grad, up_weight, order, tokens):
    step = tokens // 2
    n, k = up_weight.shape

    def kernel(order_ref, g_ref, w_ref, o_ref):
        o_ref[...] = lax.dot_general(
            g_ref[...], w_ref[...], (((1,), (1,)), ((), ())), preferred_element_type=jnp.float32
        )

    return pl.pallas_call(
        kernel,
        grid_spec=pltpu.PrefetchScalarGridSpec(
            num_scalar_prefetch=1,
            grid=(order.shape[0], 2),
            in_specs=[
                pl.BlockSpec((step, k), lambda i, j, order: (order[i] * 2 + j, 0)),
                pl.BlockSpec(memory_space=pltpu.VMEM),
            ],
            out_specs=pl.BlockSpec((step, n), lambda i, j, order: (i * 2 + j, 0)),
        ),
        out_shape=jax.ShapeDtypeStruct((order.shape[0] * tokens, n), jnp.float32),
        compiler_params=pltpu.CompilerParams(vmem_limit_bytes=54 * 1024 * 1024),
    )(order, grad, up_weight)


def local(layer_input, out_grad, up_weight):
    row = lax.axis_index("row")
    col = lax.axis_index("col")
    xl, core = row // 2 % 2, row % 2
    y, h = col // 2, col % 2
    first = core == 0
    own = row // 8 ^ y
    tokens, feats = layer_input.shape
    sub = feats // 4

    grad = lax.all_gather(out_grad, "row", axis=0, tiled=True)

    pieces = layer_input.reshape(tokens, 4, sub)
    piece = [
        [lax.dynamic_index_in_dim(pieces, 2 * v + (core ^ e), 1, keepdims=False) for e in range(2)]
        for v in range(2)
    ]
    mine = jnp.stack([piece[0][0], piece[1][0]])
    other = to_core(jnp.stack([piece[0][1], piece[1][1]]))
    both = jnp.where(first, jnp.stack([mine, other], 1), jnp.stack([other, mine], 1))
    both = move(both, lambda z, x, k, y, h: (z, x, k, z ^ y, h))
    got = [swap(pick(both, xl ^ dv), dv) for dv in range(2)]
    most = [jnp.max(jnp.abs(a)).astype(jnp.float32) for a in (out_grad, up_weight)]
    most = most_of(jnp.concatenate([jnp.broadcast_to(a, (8, 128)) for a in most]), range(3))
    *got, most = lax.optimization_barrier((*got, most))
    slab = jnp.stack([pick(jnp.stack(got), xl ^ v) for v in range(2)])
    slab = jnp.stack([slab, to_h(slab)])
    slab = jnp.stack([pick(slab, h ^ v) for v in range(2)])
    slab = jnp.stack([slab, to_y(slab, FIRST)])
    far = to_y(slab, SECOND)
    slab = jnp.stack(
        [slab[0], jnp.where(first, slab[1], far[0]), far[1], jnp.where(first, far[0], slab[1])]
    )
    slab = jnp.stack([pick(slab, own ^ v) for v in range(4)]).reshape(32 * tokens, sub)

    most = most_of(most, range(3, 8))
    most = most[:1, :1] * most[8:9, :1] * (4.0 * up_weight.shape[1])
    power = jnp.clip(14.0 - jnp.ceil(jnp.log2(most)), -126.0, 126.0)
    scale, back_scale = jnp.exp2(power), jnp.exp2(-power)

    grad, slab, scale = lax.optimization_barrier((grad, slab, scale))
    near = jnp.where(first, 1, 3)
    theirs = partial(grad, up_weight, jnp.stack([own ^ near, own ^ 2]), 8 * tokens)
    mine = partial(grad, up_weight, jnp.stack([own, own ^ near ^ 2]), 8 * tokens)

    def half(a, dv):
        a = a.reshape(2, 2, 2, 2 * tokens, sub)
        return lax.dynamic_index_in_dim(a, xl ^ dv, 2, keepdims=False)

    sums = []
    for dv in range(2):
        came = to_y(pack(half(theirs, dv), scale), FIRST).astype(jnp.float32) * back_scale
        keep = half(mine, dv) + came
        came = to_y(pack(keep[1], scale), SECOND).astype(jnp.float32) * back_scale
        sums.append(keep[0] + came)
    came = [to_h(pack(pick(a, 1 - h), scale)).astype(jnp.float32) * back_scale for a in sums]
    weight_grad = lax.dot_general(
        slab, grad, (((0,), (0,)), ((), ())), preferred_element_type=jnp.float32
    )
    weight_grad = weight_grad * (1.0 / math.sqrt(tokens * 32))
    back = []
    for dv in range(2):
        total = (pick(sums[dv], h) + came[dv]).astype(jnp.bfloat16).reshape(2, tokens, sub)
        other = to_core(pick(total, 1 - core))
        kept = pick(total, core)
        both = jnp.where(first, jnp.stack([kept, other]), jnp.stack([other, kept]))
        back.append(swap_back(both, dv))
    back = jnp.stack(back)
    back = jnp.stack([pick(back, xl ^ v) for v in range(2)])
    input_grad = jnp.concatenate([back[v, e] for v in range(2) for e in range(2)], axis=1)
    return (input_grad, weight_grad)


def solution(mesh):
    in_specs = (P("row", "col"), P("row", "col"), P("row", "col"))
    out_specs = (P("row", "col"), P("row", "col"))
    return jax.shard_map(local, mesh=mesh, in_specs=in_specs, out_specs=out_specs, check_vma=False)
```
